32 devices in a mesh: grp: 2 (over y), pix: 4 (over z), frm: 2 (over x), sub: 2 (over core).
Axes of the slice: x: 2, y: 2, z: 4, core: 2. Of those that a mesh axis runs over, the one named last changes fastest.
Arguments:
- frames: bfloat16 [8192, 2, 4096], P(('grp', 'frm', 'sub'), None, 'pix'), parts along dimension 0, may hold values from -110 to 110
Outputs:
- covariance: float32 [8192, 1024], P(('grp', 'pix', 'frm', 'sub')), parts along dimension 0
The draws below stay inside these ranges and needn't reach their ends.
There are 2 independent parts, one for each index of `grp`. The reference program is written for one: setup_inputs(seed, part) draws one part's arguments, and reference() takes and returns one part's arrays. A program takes and returns all parts, laid end to end along the dimension named above; each array names one. Nothing has to cross between parts.
All inputs are finite; a program needn't handle non-finite values.
Results may differ from the reference program's by a relative error of at most 0.0003.
Values may be sent and summed in bfloat16 or wider, within the bound.
A program may use at most 64 MiB of HBM per device.

```python
import math
import jax
import jax.numpy as jnp
from jax import lax

BLOCK = 1024
FRAMES = 4096
PIXHALF = 4096
OFFSET = 1
N_PIX = 4


def draw_frames(key, part):
    key = jax.random.fold_in(key, 7)
    keys = jax.random.split(key, 5)
    pixel_shape = (2, PIXHALF)
    gains = jnp.exp(jax.random.uniform(keys[0], pixel_shape, jnp.float32, math.log(0.3), math.log(3.0)))
    noise = 4.0 * jnp.clip(jax.random.normal(keys[4], (FRAMES, 2, PIXHALF), jnp.float32), -4.0, 4.0)
    spread = 0.25
    level = jax.random.uniform(keys[1], pixel_shape, jnp.float32, 1.0, 3.0)
    drift = 1.0 + 2.0 * jnp.arange(FRAMES, dtype=jnp.float32) / max(FRAMES - 1, 1)
    shared = jnp.clip(jax.random.normal(keys[2], (FRAMES,), jnp.float32), -4.0, 4.0)
    couple = jnp.clip(spread * jax.random.normal(keys[3], pixel_shape, jnp.float32), -1.0, 1.0)
    values = level[None] * drift[:, None, None] + noise + 2.4 * couple[None] * shared[:, None, None]
    return (gains[None] * values).astype(jnp.bfloat16)


def setup_inputs(seed: int = 0, part: int = 0) -> dict:
    seeds = jax.random.split(jax.random.key(seed), 2)
    part_splits = jax.random.split(jax.random.fold_in(seeds[1], part), 2)
    frames = draw_frames(jax.random.fold_in(jax.random.fold_in(seeds[1], part), 71), part)
    return dict(frames=frames)


def reference(frames):
    lower = frames[:, 0, :].reshape(FRAMES, N_PIX, BLOCK)
    upper = jnp.roll(frames[:, 1, :].reshape(FRAMES, N_PIX, BLOCK), OFFSET, axis=1)
    lower = jnp.swapaxes(lower, 0, 1)
    upper = jnp.swapaxes(upper, 0, 1)
    mean_lower = jnp.sum(lower.astype(jnp.float32), axis=1) / FRAMES
    mean_upper = jnp.sum(upper.astype(jnp.float32), axis=1) / FRAMES

    def one_pair(pair):
        left, right = pair
        return jnp.dot(left.T, right, preferred_element_type=jnp.float32)

    grams = lax.map(one_pair, (lower, upper))
    tiles = grams / FRAMES - mean_lower[:, :, None] * mean_upper[:, None, :]
    return tiles.reshape(N_PIX * BLOCK, BLOCK)
```

```python
import functools

import jax
import jax.numpy as jnp
from jax import lax
from jax.experimental import pallas as pl
from jax.experimental.pallas import tpu as pltpu
from jax.sharding import PartitionSpec as P

MESH = pl.DeviceIdType.MESH
WIDTH = 128
GROUP = 128
SUMS = 8


def selector(half):
    row = lax.broadcasted_iota(jnp.int32, (GROUP, 2 * GROUP), 0)
    column = lax.broadcasted_iota(jnp.int32, (GROUP, 2 * GROUP), 1)
    return jnp.where(column == 2 * row + half, 1.0, 0.0).astype(jnp.bfloat16)


def product(left, right):
    return jnp.dot(left, right, preferred_element_type=jnp.float32)


def kernel(
    n_pix, n_frm, offset,
    frames_ref, out_ref,
    mixed, upper, visitor, twin, lower, lower_twin, own, outgoing, incoming,
    sums_out, sums_in, mean_lower,
    load_sem, z_send, z_recv, f_send, f_recv, x_send, x_recv, l_send, l_recv, s_send, s_recv,
):
    frame_count, _, block = frames_ref.shape
    chunks = block // WIDTH
    rows = out_ref.shape[0]
    total = frame_count * n_frm * 2
    pix, frm, sub = lax.axis_index("pix"), lax.axis_index("frm"), lax.axis_index("sub")
    ahead = {"pix": lax.rem(pix + offset, n_pix)}
    behind = {"pix": lax.rem(pix + n_pix - offset, n_pix)}
    sibling = {"sub": 1 - sub}
    peers = [lax.rem(frm + 1 + k, n_frm) for k in range(n_frm - 1)]

    def load(c):
        columns = pl.ds(c * WIDTH, WIDTH)
        return pltpu.make_async_copy(frames_ref.at[:, :, columns], mixed.at[c], load_sem.at[c])

    def remote(src, dst, send, recv, device):
        return pltpu.make_async_remote_copy(
            src_ref=src, dst_ref=dst, send_sem=send, recv_sem=recv, device_id=device, device_id_type=MESH
        )

    def pass_on(c):
        return remote(upper.at[c], visitor.at[c], z_send.at[c], z_recv.at[c], ahead)

    def share(c):
        return remote(visitor.at[c], twin.at[c], f_send.at[c], f_recv.at[c], sibling)

    def give(c, k):
        return remote(
            outgoing.at[c, k], incoming.at[c, k], x_send.at[c, k], x_recv.at[c, k], {"frm": peers[k]}
        )

    def rows_of(f, s):
        return pl.ds(pl.multiple_of((f * 2 + s) * rows, rows), rows)

    def share_lower(f):
        return remote(lower.at[rows_of(f, 1 - sub)], lower_twin.at[f], l_send.at[f], l_recv.at[f], sibling)

    def give_sums(k):
        return remote(sums_out.at[k], sums_in.at[k], s_send.at[k], s_recv.at[k], {"frm": peers[k]})

    load(0).start()
    load(1).start()
    barrier = pltpu.get_barrier_semaphore()
    neighbours = [ahead, behind, sibling] + [{"frm": f} for f in peers]
    for device in neighbours:
        pl.semaphore_signal(barrier, inc=1, device_id=device, device_id_type=MESH)

    pick_upper, pick_lower = selector(1), selector(0)
    for c in range(chunks):
        load(c).wait()
        if c + 2 < chunks:
            load(c + 2).start()
        for g in range(frame_count // GROUP):
            part = mixed[c, pl.ds(g * GROUP, GROUP)].reshape(2 * GROUP, WIDTH)
            upper[c, pl.ds(g * GROUP, GROUP)] = product(pick_upper, part).astype(jnp.bfloat16)
        if c == 0:
            pl.semaphore_wait(barrier, len(neighbours))
        pass_on(c).start()

    def separate(c, _):
        for g in range(frame_count // GROUP):
            part = mixed[c, pl.ds(g * GROUP, GROUP)].reshape(2 * GROUP, WIDTH)
            lower[pl.ds(pl.multiple_of(c * WIDTH, WIDTH), WIDTH), pl.ds(g * GROUP, GROUP)] = (
                product(pick_lower, part).T.astype(jnp.bfloat16)
            )
        return 0

    lax.fori_loop(0, chunks, separate, 0)
    for f in range(n_frm):
        share_lower(f).start()
    for f in range(n_frm):
        share_lower(f).wait_recv()
    ones = jnp.ones((frame_count, 128), jnp.bfloat16)
    for k in range(n_frm - 1):
        sums_out[k] = product(lower[rows_of(peers[k], sub)], ones) + product(lower_twin[peers[k]], ones)
        give_sums(k).start()
    own_sums = product(lower[rows_of(frm, sub)], ones) + product(lower_twin[frm], ones)
    for k in range(n_frm - 1):
        give_sums(k).wait_recv()
        own_sums += sums_in[k]
    mean_lower[...] = own_sums / total

    ones_row = jnp.ones((16, frame_count), jnp.bfloat16)

    def finish(c):
        gram = own[c]
        for k in range(n_frm - 1):
            give(c, k).wait_recv()
            gram += incoming[c, k]
        mean_upper = gram[rows : rows + 1] / total
        out_ref[:, pl.ds(pl.multiple_of(c * WIDTH, WIDTH), WIDTH)] = (
            gram[:rows] / total - mean_lower[...] * mean_upper
        )

    def step(c, _):
        pass_on(c).wait_recv()
        share(c).start()

        def pair(f):
            return product(lower[rows_of(f, sub)], visitor[c]) + product(lower_twin[f], twin[c])

        share(c).wait_recv()
        column_sums = (product(ones_row, visitor[c]) + product(ones_row, twin[c]))[:SUMS]
        for k in range(n_frm - 1):
            outgoing[c, k, :rows] = pair(peers[k])
            outgoing[c, k, rows:] = column_sums
            give(c, k).start()
        own[c, :rows] = pair(frm)
        own[c, rows:] = column_sums

        @pl.when(c > 0)
        def _():
            finish(c - 1)

        return 0

    lax.fori_loop(0, chunks, step, 0)
    finish(chunks - 1)

    for f in range(n_frm):
        share_lower(f).wait_send()
    for k in range(n_frm - 1):
        give_sums(k).wait_send()

    def drain(c, _):
        pass_on(c).wait_send()
        share(c).wait_send()
        for k in range(n_frm - 1):
            give(c, k).wait_send()
        return 0

    lax.fori_loop(0, chunks, drain, 0)


def shards(n_pix, n_frm, n_sub, frames):
    frame_count, _, block = frames.shape
    assert n_sub == 2
    chunks, rows, others = block // WIDTH, block // (n_frm * 2), n_frm - 1
    f32, bf16 = jnp.float32, jnp.bfloat16
    dma = pltpu.SemaphoreType.DMA
    return pl.pallas_call(
        functools.partial(kernel, n_pix, n_frm, max(n_pix // 4, 1)),
        out_shape=jax.ShapeDtypeStruct((rows, block), f32),
        in_specs=[pl.BlockSpec(memory_space=pl.ANY)],
        out_specs=pl.BlockSpec(memory_space=pltpu.VMEM),
        scratch_shapes=[
            pltpu.VMEM((chunks, frame_count, 2, WIDTH), bf16),
            pltpu.VMEM((chunks, frame_count, WIDTH), bf16),
            pltpu.VMEM((chunks, frame_count, WIDTH), bf16),
            pltpu.VMEM((chunks, frame_count, WIDTH), bf16),
            pltpu.VMEM((block, frame_count), bf16),
            pltpu.VMEM((n_frm, rows, frame_count), bf16),
            pltpu.VMEM((chunks, rows + SUMS, WIDTH), f32),
            pltpu.VMEM((chunks, others, rows + SUMS, WIDTH), f32),
            pltpu.VMEM((chunks, others, rows + SUMS, WIDTH), f32),
            pltpu.VMEM((others, rows, 128), f32),
            pltpu.VMEM((others, rows, 128), f32),
            pltpu.VMEM((rows, 128), f32),
            dma((chunks,)), dma((chunks,)), dma((chunks,)), dma((chunks,)), dma((chunks,)),
            dma((chunks, others)), dma((chunks, others)),
            dma((n_frm,)), dma((n_frm,)), dma((others,)), dma((others,)),
        ],
        compiler_params=pltpu.CompilerParams(
            collective_id=0, has_side_effects=True, vmem_limit_bytes=60 << 20
        ),
        cost_estimate=pl.CostEstimate(
            flops=2 * frame_count * block * block, bytes_accessed=4 * frame_count * block, transcendentals=0
        ),
    )(frames)


def solution(mesh):
    shape = mesh.shape
    return jax.shard_map(
        functools.partial(shards, shape["pix"], shape["frm"], shape["sub"]),
        mesh=mesh,
        in_specs=(P(("grp", "frm", "sub"), None, "pix"),),
        out_specs=P(("grp", "pix", "frm", "sub"), None),
        check_vma=False,
    )
```

```python
import functools

import jax
import jax.numpy as jnp
from jax import lax
from jax.experimental import pallas as pl
from jax.experimental.pallas import tpu as pltpu
from jax.sharding import PartitionSpec as P

MESH = pl.DeviceIdType.MESH
WIDTH = 128
GROUP = 128
PIECES = 4
SUMS = 8


def selector(half):
    row = lax.broadcasted_iota(jnp.int32, (GROUP, 2 * GROUP), 0)
    column = lax.broadcasted_iota(jnp.int32, (GROUP, 2 * GROUP), 1)
    return jnp.where(column == 2 * row + half, 1.0, 0.0).astype(jnp.bfloat16)


def product(left, right):
    return jnp.dot(left, right, preferred_element_type=jnp.float32)


def kernel(
    n_pix, n_frm, offset,
    frames_ref, out_ref,
    mixed, upper, visitor, twin, lower, lower_twin, own, outgoing, incoming,
    sums_out, sums_in, mean_lower,
    load_sem, piece_load, piece_send, piece_recv, z_send, z_recv, f_send, f_recv, x_send, x_recv, l_send, l_recv, s_send, s_recv,
):
    frame_count, _, block = frames_ref.shape
    chunks = block // WIDTH
    rows = out_ref.shape[0]
    total = frame_count * n_frm * 2
    pix, frm, sub = lax.axis_index("pix"), lax.axis_index("frm"), lax.axis_index("sub")
    ahead = {"pix": lax.rem(pix + offset, n_pix)}
    behind = {"pix": lax.rem(pix + n_pix - offset, n_pix)}
    sibling = {"sub": 1 - sub}
    peers = [lax.rem(frm + 1 + k, n_frm) for k in range(n_frm - 1)]

    piece = frame_count // PIECES

    def load(c):
        columns = pl.ds(c * WIDTH, WIDTH)
        return pltpu.make_async_copy(frames_ref.at[:, :, columns], mixed.at[c], load_sem.at[c])

    def load_piece(i):
        run = pl.ds(i * piece, piece)
        return pltpu.make_async_copy(frames_ref.at[run, :, pl.ds(0, WIDTH)], mixed.at[0, run], piece_load.at[i])

    def remote(src, dst, send, recv, device):
        return pltpu.make_async_remote_copy(
            src_ref=src, dst_ref=dst, send_sem=send, recv_sem=recv, device_id=device, device_id_type=MESH
        )

    def pass_on(c):
        return remote(upper.at[c], visitor.at[c], z_send.at[c], z_recv.at[c], ahead)

    def pass_on_piece(i):
        run = pl.ds(i * piece, piece)
        return remote(upper.at[0, run], visitor.at[0, run], piece_send.at[i], piece_recv.at[i], ahead)

    def share(c):
        return remote(visitor.at[c], twin.at[c], f_send.at[c], f_recv.at[c], sibling)

    def give(c, k):
        return remote(
            outgoing.at[c, k], incoming.at[c, k], x_send.at[c, k], x_recv.at[c, k], {"frm": peers[k]}
        )

    def rows_of(f, s):
        return pl.ds(pl.multiple_of((f * 2 + s) * rows, rows), rows)

    def share_lower(f):
        return remote(lower.at[rows_of(f, 1 - sub)], lower_twin.at[f], l_send.at[f], l_recv.at[f], sibling)

    def give_sums(k):
        return remote(sums_out.at[k], sums_in.at[k], s_send.at[k], s_recv.at[k], {"frm": peers[k]})

    for i in range(PIECES):
        load_piece(i).start()
    load(1).start()
    barrier = pltpu.get_barrier_semaphore()
    neighbours = [ahead, behind, sibling] + [{"frm": f} for f in peers]
    for device in neighbours:
        pl.semaphore_signal(barrier, inc=1, device_id=device, device_id_type=MESH)

    pick_upper, pick_lower = selector(1), selector(0)

    def separate_upper(c, first, last):
        for g in range(first // GROUP, last // GROUP):
            part = mixed[c, pl.ds(g * GROUP, GROUP)].reshape(2 * GROUP, WIDTH)
            upper[c, pl.ds(g * GROUP, GROUP)] = product(pick_upper, part).astype(jnp.bfloat16)

    for i in range(PIECES):
        load_piece(i).wait()
        separate_upper(0, i * piece, (i + 1) * piece)
        if i == 0:
            pl.semaphore_wait(barrier, len(neighbours))
        pass_on_piece(i).start()
    load(2).start()
    for c in range(1, chunks):
        load(c).wait()
        if c + 2 < chunks:
            load(c + 2).start()
        separate_upper(c, 0, frame_count)
        pass_on(c).start()

    def separate(c, _):
        for g in range(frame_count // GROUP):
            part = mixed[c, pl.ds(g * GROUP, GROUP)].reshape(2 * GROUP, WIDTH)
            lower[pl.ds(pl.multiple_of(c * WIDTH, WIDTH), WIDTH), pl.ds(g * GROUP, GROUP)] = (
                product(pick_lower, part).T.astype(jnp.bfloat16)
            )
        return 0

    lax.fori_loop(0, chunks, separate, 0)
    for f in range(n_frm):
        share_lower(f).start()
    for f in range(n_frm):
        share_lower(f).wait_recv()
    ones = jnp.ones((frame_count, 128), jnp.bfloat16)
    for k in range(n_frm - 1):
        sums_out[k] = product(lower[rows_of(peers[k], sub)], ones) + product(lower_twin[peers[k]], ones)
        give_sums(k).start()
    own_sums = product(lower[rows_of(frm, sub)], ones) + product(lower_twin[frm], ones)
    for k in range(n_frm - 1):
        give_sums(k).wait_recv()
        own_sums += sums_in[k]
    mean_lower[...] = own_sums / total

    ones_row = jnp.ones((16, frame_count), jnp.bfloat16)

    def finish(c):
        gram = own[c]
        for k in range(n_frm - 1):
            give(c, k).wait_recv()
            gram += incoming[c, k]
        mean_upper = gram[rows : rows + 1] / total
        out_ref[:, pl.ds(pl.multiple_of(c * WIDTH, WIDTH), WIDTH)] = (
            gram[:rows] / total - mean_lower[...] * mean_upper
        )

    def step(c, _):
        @pl.when(c == 0)
        def _():
            for i in range(PIECES):
                pass_on_piece(i).wait_recv()

        @pl.when(c > 0)
        def _():
            pass_on(c).wait_recv()

        share(c).start()

        def pair(f):
            return product(lower[rows_of(f, sub)], visitor[c]) + product(lower_twin[f], twin[c])

        share(c).wait_recv()
        column_sums = (product(ones_row, visitor[c]) + product(ones_row, twin[c]))[:SUMS]
        for k in range(n_frm - 1):
            outgoing[c, k, :rows] = pair(peers[k])
            outgoing[c, k, rows:] = column_sums
            give(c, k).start()
        own[c, :rows] = pair(frm)
        own[c, rows:] = column_sums

        @pl.when(c > 0)
        def _():
            finish(c - 1)

        return 0

    lax.fori_loop(0, chunks, step, 0)
    finish(chunks - 1)

    for f in range(n_frm):
        share_lower(f).wait_send()
    for k in range(n_frm - 1):
        give_sums(k).wait_send()

    def drain(c, _):
        @pl.when(c == 0)
        def _():
            for i in range(PIECES):
                pass_on_piece(i).wait_send()

        @pl.when(c > 0)
        def _():
            pass_on(c).wait_send()

        share(c).wait_send()
        for k in range(n_frm - 1):
            give(c, k).wait_send()
        return 0

    lax.fori_loop(0, chunks, drain, 0)


def shards(n_pix, n_frm, n_sub, frames):
    frame_count, _, block = frames.shape
    assert n_sub == 2 and block > 2 * WIDTH
    chunks, rows, others = block // WIDTH, block // (n_frm * 2), n_frm - 1
    f32, bf16 = jnp.float32, jnp.bfloat16
    dma = pltpu.SemaphoreType.DMA
    return pl.pallas_call(
        functools.partial(kernel, n_pix, n_frm, max(n_pix // 4, 1)),
        out_shape=jax.ShapeDtypeStruct((rows, block), f32),
        in_specs=[pl.BlockSpec(memory_space=pl.ANY)],
        out_specs=pl.BlockSpec(memory_space=pltpu.VMEM),
        scratch_shapes=[
            pltpu.VMEM((chunks, frame_count, 2, WIDTH), bf16),
            pltpu.VMEM((chunks, frame_count, WIDTH), bf16),
            pltpu.VMEM((chunks, frame_count, WIDTH), bf16),
            pltpu.VMEM((chunks, frame_count, WIDTH), bf16),
            pltpu.VMEM((block, frame_count), bf16),
            pltpu.VMEM((n_frm, rows, frame_count), bf16),
            pltpu.VMEM((chunks, rows + SUMS, WIDTH), f32),
            pltpu.VMEM((chunks, others, rows + SUMS, WIDTH), f32),
            pltpu.VMEM((chunks, others, rows + SUMS, WIDTH), f32),
            pltpu.VMEM((others, rows, 128), f32),
            pltpu.VMEM((others, rows, 128), f32),
            pltpu.VMEM((rows, 128), f32),
            dma((chunks,)), dma((PIECES,)), dma((PIECES,)), dma((PIECES,)),
            dma((chunks,)), dma((chunks,)), dma((chunks,)), dma((chunks,)),
            dma((chunks, others)), dma((chunks, others)),
            dma((n_frm,)), dma((n_frm,)), dma((others,)), dma((others,)),
        ],
        compiler_params=pltpu.CompilerParams(
            collective_id=0, has_side_effects=True, vmem_limit_bytes=51 << 20
        ),
        cost_estimate=pl.CostEstimate(
            flops=2 * frame_count * block * block, bytes_accessed=4 * frame_count * block, transcendentals=0
        ),
    )(frames)


def solution(mesh):
    shape = mesh.shape
    return jax.shard_map(
        functools.partial(shards, shape["pix"], shape["frm"], shape["sub"]),
        mesh=mesh,
        in_specs=(P(("grp", "frm", "sub"), None, "pix"),),
        out_specs=P(("grp", "pix", "frm", "sub"), None),
        check_vma=False,
    )
```

```python
import functools

import jax
import jax.numpy as jnp
from jax import lax
from jax.experimental import pallas as pl
from jax.experimental.pallas import tpu as pltpu
from jax.sharding import PartitionSpec as P

MESH = pl.DeviceIdType.MESH
WIDTH = 128
GROUP = 128
PIECES = 4
SUMS = 8


def selector(half):
    row = lax.broadcasted_iota(jnp.int32, (GROUP, 2 * GROUP), 0)
    column = lax.broadcasted_iota(jnp.int32, (GROUP, 2 * GROUP), 1)
    return jnp.where(column == 2 * row + half, 1.0, 0.0).astype(jnp.bfloat16)


def product(left, right):
    return jnp.dot(left, right, preferred_element_type=jnp.float32)


def swapped(value):
    return pltpu.roll(value, WIDTH // 2, 1)


def joined(left, right):
    lane = lax.broadcasted_iota(jnp.int32, left.shape, 1)
    return jnp.where(lane < WIDTH // 2, left, right)


def kernel(
    n_pix, n_frm, offset,
    frames_ref, out_ref,
    mixed, upper, visitor, twin, lower, lower_twin, own, outgoing, incoming,
    sums_out, sums_in, mean_lower,
    upper_half, visitor_half, twin_half, own_half, outgoing_half, incoming_half,
    load_sem, piece_load, piece_send, piece_recv, z_send, z_recv, f_send, f_recv, x_send, x_recv, l_send, l_recv, s_send, s_recv,
    hz_send, hz_recv, hf_send, hf_recv, hx_send, hx_recv,
):
    frame_count, _, block = frames_ref.shape
    chunks = block // WIDTH
    rows = out_ref.shape[0]
    total = frame_count * n_frm * 2
    pix, frm, sub = lax.axis_index("pix"), lax.axis_index("frm"), lax.axis_index("sub")
    ahead = {"pix": lax.rem(pix + offset, n_pix)}
    behind = {"pix": lax.rem(pix + n_pix - offset, n_pix)}
    sibling = {"sub": 1 - sub}
    peers = [lax.rem(frm + 1 + k, n_frm) for k in range(n_frm - 1)]

    piece = frame_count // PIECES

    def load(c):
        columns = pl.ds(c * WIDTH, WIDTH)
        return pltpu.make_async_copy(frames_ref.at[:, :, columns], mixed.at[c], load_sem.at[c])

    def load_piece(i):
        run = pl.ds(i * piece, piece)
        return pltpu.make_async_copy(frames_ref.at[run, :, pl.ds(0, WIDTH)], mixed.at[0, run], piece_load.at[i])

    def remote(src, dst, send, recv, device):
        return pltpu.make_async_remote_copy(
            src_ref=src, dst_ref=dst, send_sem=send, recv_sem=recv, device_id=device, device_id_type=MESH
        )

    def pass_on(c):
        return remote(upper.at[c], visitor.at[c], z_send.at[c], z_recv.at[c], ahead)

    def pass_on_piece(i):
        run = pl.ds(i * piece, piece)
        return remote(upper.at[0, run], visitor.at[0, run], piece_send.at[i], piece_recv.at[i], ahead)

    def share(c):
        return remote(visitor.at[c], twin.at[c], f_send.at[c], f_recv.at[c], sibling)

    def give(c, k):
        return remote(
            outgoing.at[c, k], incoming.at[c, k], x_send.at[c, k], x_recv.at[c, k], {"frm": peers[k]}
        )

    def pass_on_half(h):
        return remote(upper_half.at[h], visitor_half.at[h], hz_send.at[h], hz_recv.at[h], ahead)

    def share_half(h):
        return remote(visitor_half.at[h], twin_half.at[h], hf_send.at[h], hf_recv.at[h], sibling)

    def give_half(h, k):
        return remote(
            outgoing_half.at[h, k], incoming_half.at[h, k], hx_send.at[h, k], hx_recv.at[h, k], {"frm": peers[k]}
        )

    def rows_of(f, s):
        return pl.ds(pl.multiple_of((f * 2 + s) * rows, rows), rows)

    def share_lower(f):
        return remote(lower.at[rows_of(f, 1 - sub)], lower_twin.at[f], l_send.at[f], l_recv.at[f], sibling)

    def give_sums(k):
        return remote(sums_out.at[k], sums_in.at[k], s_send.at[k], s_recv.at[k], {"frm": peers[k]})

    for i in range(PIECES):
        load_piece(i).start()
    load(1).start()
    barrier = pltpu.get_barrier_semaphore()
    neighbours = [ahead, behind, sibling] + [{"frm": f} for f in peers]
    for device in neighbours:
        pl.semaphore_signal(barrier, inc=1, device_id=device, device_id_type=MESH)

    pick_upper, pick_lower = selector(1), selector(0)

    def separate_upper(c, first, last):
        for g in range(first // GROUP, last // GROUP):
            part = mixed[c, pl.ds(g * GROUP, GROUP)].reshape(2 * GROUP, WIDTH)
            upper[c, pl.ds(g * GROUP, GROUP)] = product(pick_upper, part).astype(jnp.bfloat16)

    for i in range(PIECES):
        load_piece(i).wait()
        separate_upper(0, i * piece, (i + 1) * piece)
        if i == 0:
            pl.semaphore_wait(barrier, len(neighbours))
        pass_on_piece(i).start()
    load(2).start()
    for c in range(1, chunks - 1):
        load(c).wait()
        if c + 2 < chunks:
            load(c + 2).start()
        separate_upper(c, 0, frame_count)
        pass_on(c).start()
    last, middle, half_rows = chunks - 1, frame_count // 2, rows // 2
    load(last).wait()
    for g in range(middle // GROUP):
        early, late = (
            product(pick_upper, mixed[last, pl.ds(first, GROUP)].reshape(2 * GROUP, WIDTH))
            for first in (g * GROUP, middle + g * GROUP)
        )
        upper_half[0, pl.ds(g * GROUP, GROUP)] = joined(early, swapped(late)).astype(jnp.bfloat16)
        upper_half[1, pl.ds(g * GROUP, GROUP)] = joined(swapped(early), late).astype(jnp.bfloat16)
    for h in range(2):
        pass_on_half(h).start()

    def separate(c, _):
        for g in range(frame_count // GROUP):
            part = mixed[c, pl.ds(g * GROUP, GROUP)].reshape(2 * GROUP, WIDTH)
            lower[pl.ds(pl.multiple_of(c * WIDTH, WIDTH), WIDTH), pl.ds(g * GROUP, GROUP)] = (
                product(pick_lower, part).T.astype(jnp.bfloat16)
            )
        return 0

    lax.fori_loop(0, chunks, separate, 0)
    for f in range(n_frm):
        share_lower(f).start()
    for f in range(n_frm):
        share_lower(f).wait_recv()
    ones = jnp.ones((frame_count, 128), jnp.bfloat16)
    for k in range(n_frm - 1):
        sums_out[k] = product(lower[rows_of(peers[k], sub)], ones) + product(lower_twin[peers[k]], ones)
        give_sums(k).start()
    own_sums = product(lower[rows_of(frm, sub)], ones) + product(lower_twin[frm], ones)
    for k in range(n_frm - 1):
        give_sums(k).wait_recv()
        own_sums += sums_in[k]
    mean_lower[...] = own_sums / total

    ones_row = jnp.ones((16, frame_count), jnp.bfloat16)

    def finish(c):
        gram = own[c]
        for k in range(n_frm - 1):
            give(c, k).wait_recv()
            gram += incoming[c, k]
        mean_upper = gram[rows : rows + 1] / total
        out_ref[:, pl.ds(pl.multiple_of(c * WIDTH, WIDTH), WIDTH)] = (
            gram[:rows] / total - mean_lower[...] * mean_upper
        )

    def step(c, _):
        @pl.when(c == 0)
        def _():
            for i in range(PIECES):
                pass_on_piece(i).wait_recv()

        @pl.when(c > 0)
        def _():
            pass_on(c).wait_recv()

        share(c).start()

        def pair(f):
            return product(lower[rows_of(f, sub)], visitor[c]) + product(lower_twin[f], twin[c])

        share(c).wait_recv()
        column_sums = (product(ones_row, visitor[c]) + product(ones_row, twin[c]))[:SUMS]
        for k in range(n_frm - 1):
            outgoing[c, k, :rows] = pair(peers[k])
            outgoing[c, k, rows:] = column_sums
            give(c, k).start()
        own[c, :rows] = pair(frm)
        own[c, rows:] = column_sums

        @pl.when(c > 0)
        def _():
            finish(c - 1)

        return 0

    lax.fori_loop(0, last, step, 0)

    def step_half(h):
        pass_on_half(h).wait_recv()
        share_half(h).start()

        def pair(f):
            def over(run):
                return product(lower[rows_of(f, sub), run], visitor_half[h]) + product(
                    lower_twin[f, :, run], twin_half[h]
                )

            early, late = over(slice(0, middle)), over(slice(middle, frame_count))
            return joined(
                early[:half_rows] + swapped(late[:half_rows]), swapped(early[half_rows:]) + late[half_rows:]
            )

        share_half(h).wait_recv()
        column_sums = (
            product(ones_row[:, :middle], visitor_half[h]) + product(ones_row[:, :middle], twin_half[h])
        )[:SUMS]
        column_sums = column_sums + swapped(column_sums)
        for k in range(n_frm - 1):
            outgoing_half[h, k, :half_rows] = pair(peers[k])
            outgoing_half[h, k, half_rows:] = column_sums
            give_half(h, k).start()
        own_half[h, :half_rows] = pair(frm)
        own_half[h, half_rows:] = column_sums

    def finished_half(h):
        gram = own_half[h]
        for k in range(n_frm - 1):
            give_half(h, k).wait_recv()
            gram += incoming_half[h, k]
        mean_upper = gram[half_rows : half_rows + 1] / total
        means = joined(mean_lower[:half_rows], mean_lower[half_rows:])
        return gram[:half_rows] / total - means * mean_upper

    step_half(0)
    finish(last - 1)
    step_half(1)
    first_half = finished_half(0)
    second_half = finished_half(1)
    columns = pl.ds(last * WIDTH, WIDTH)
    out_ref[:half_rows, columns] = joined(first_half, swapped(second_half))
    out_ref[half_rows:, columns] = joined(swapped(first_half), second_half)

    for f in range(n_frm):
        share_lower(f).wait_send()
    for k in range(n_frm - 1):
        give_sums(k).wait_send()

    def drain(c, _):
        @pl.when(c == 0)
        def _():
            for i in range(PIECES):
                pass_on_piece(i).wait_send()

        @pl.when(c > 0)
        def _():
            pass_on(c).wait_send()

        share(c).wait_send()
        for k in range(n_frm - 1):
            give(c, k).wait_send()
        return 0

    lax.fori_loop(0, last, drain, 0)
    for h in range(2):
        pass_on_half(h).wait_send()
        share_half(h).wait_send()
        for k in range(n_frm - 1):
            give_half(h, k).wait_send()


def shards(n_pix, n_frm, n_sub, frames):
    frame_count, _, block = frames.shape
    assert n_sub == 2 and block > 2 * WIDTH
    chunks, rows, others = block // WIDTH, block // (n_frm * 2), n_frm - 1
    f32, bf16 = jnp.float32, jnp.bfloat16
    dma = pltpu.SemaphoreType.DMA
    return pl.pallas_call(
        functools.partial(kernel, n_pix, n_frm, max(n_pix // 4, 1)),
        out_shape=jax.ShapeDtypeStruct((rows, block), f32),
        in_specs=[pl.BlockSpec(memory_space=pl.ANY)],
        out_specs=pl.BlockSpec(memory_space=pltpu.VMEM),
        scratch_shapes=[
            pltpu.VMEM((chunks, frame_count, 2, WIDTH), bf16),
            pltpu.VMEM((chunks, frame_count, WIDTH), bf16),
            pltpu.VMEM((chunks, frame_count, WIDTH), bf16),
            pltpu.VMEM((chunks, frame_count, WIDTH), bf16),
            pltpu.VMEM((block, frame_count), bf16),
            pltpu.VMEM((n_frm, rows, frame_count), bf16),
            pltpu.VMEM((chunks, rows + SUMS, WIDTH), f32),
            pltpu.VMEM((chunks, others, rows + SUMS, WIDTH), f32),
            pltpu.VMEM((chunks, others, rows + SUMS, WIDTH), f32),
            pltpu.VMEM((others, rows, 128), f32),
            pltpu.VMEM((others, rows, 128), f32),
            pltpu.VMEM((rows, 128), f32),
            pltpu.VMEM((2, frame_count // 2, WIDTH), bf16),
            pltpu.VMEM((2, frame_count // 2, WIDTH), bf16),
            pltpu.VMEM((2, frame_count // 2, WIDTH), bf16),
            pltpu.VMEM((2, rows // 2 + SUMS, WIDTH), f32),
            pltpu.VMEM((2, others, rows // 2 + SUMS, WIDTH), f32),
            pltpu.VMEM((2, others, rows // 2 + SUMS, WIDTH), f32),
            dma((chunks,)), dma((PIECES,)), dma((PIECES,)), dma((PIECES,)),
            dma((chunks,)), dma((chunks,)), dma((chunks,)), dma((chunks,)),
            dma((chunks, others)), dma((chunks, others)),
            dma((n_frm,)), dma((n_frm,)), dma((others,)), dma((others,)),
            dma((2,)), dma((2,)), dma((2,)), dma((2,)), dma((2, others)), dma((2, others)),
        ],
        compiler_params=pltpu.CompilerParams(
            collective_id=0, has_side_effects=True, vmem_limit_bytes=51 << 20
        ),
        cost_estimate=pl.CostEstimate(
            flops=2 * frame_count * block * block, bytes_accessed=4 * frame_count * block, transcendentals=0
        ),
    )(frames)


def solution(mesh):
    shape = mesh.shape
    return jax.shard_map(
        functools.partial(shards, shape["pix"], shape["frm"], shape["sub"]),
        mesh=mesh,
        in_specs=(P(("grp", "frm", "sub"), None, "pix"),),
        out_specs=P(("grp", "pix", "frm", "sub"), None),
        check_vma=False,
    )
```

```python
import functools

import jax
import jax.numpy as jnp
from jax import lax
from jax.experimental import pallas as pl
from jax.experimental.pallas import tpu as pltpu
from jax.sharding import PartitionSpec as P

MESH = pl.DeviceIdType.MESH
WIDTH = 128
GROUP = 128
PIECES = 4
SUMS = 8


def selector(half):
    row = lax.broadcasted_iota(jnp.int32, (GROUP, 2 * GROUP), 0)
    column = lax.broadcasted_iota(jnp.int32, (GROUP, 2 * GROUP), 1)
    return jnp.where(column == 2 * row + half, 1.0, 0.0).astype(jnp.bfloat16)


def product(left, right):
    return jnp.dot(left, right, preferred_element_type=jnp.float32)


def swapped(value):
    return pltpu.roll(value, WIDTH // 2, 1)


def joined(left, right):
    lane = lax.broadcasted_iota(jnp.int32, left.shape, 1)
    return jnp.where(lane < WIDTH // 2, left, right)


def kernel(
    n_pix, n_frm, offset,
    frames_ref, out_ref,
    mixed, upper, visitor, twin, lower, lower_twin, own, outgoing, incoming,
    sums_out, sums_in, mean_lower,
    upper_half, visitor_half, twin_half, own_half, outgoing_half, incoming_half,
    load_sem, piece_load, piece_send, piece_recv, z_send, z_recv, f_send, f_recv, x_send, x_recv, l_send, l_recv, s_send, s_recv,
    hz_send, hz_recv, hf_send, hf_recv, hx_send, hx_recv,
):
    frame_count, _, block = frames_ref.shape
    chunks = block // WIDTH
    rows = out_ref.shape[0]
    total = frame_count * n_frm * 2
    pix, frm, sub = lax.axis_index("pix"), lax.axis_index("frm"), lax.axis_index("sub")
    ahead = {"pix": lax.rem(pix + offset, n_pix)}
    behind = {"pix": lax.rem(pix + n_pix - offset, n_pix)}
    sibling = {"sub": 1 - sub}
    peers = [lax.rem(frm + 1 + k, n_frm) for k in range(n_frm - 1)]

    piece = frame_count // PIECES

    def load(c):
        columns = pl.ds(c * WIDTH, WIDTH)
        return pltpu.make_async_copy(frames_ref.at[:, :, columns], mixed.at[c], load_sem.at[c])

    def load_piece(i):
        run = pl.ds(i * piece, piece)
        return pltpu.make_async_copy(frames_ref.at[run, :, pl.ds(0, WIDTH)], mixed.at[0, run], piece_load.at[i])

    def remote(src, dst, send, recv, device):
        return pltpu.make_async_remote_copy(
            src_ref=src, dst_ref=dst, send_sem=send, recv_sem=recv, device_id=device, device_id_type=MESH
        )

    def pass_on(c):
        return remote(upper.at[c], visitor.at[c], z_send.at[c], z_recv.at[c], ahead)

    def pass_on_piece(i):
        run = pl.ds(i * piece, piece)
        return remote(upper.at[0, run], visitor.at[0, run], piece_send.at[i], piece_recv.at[i], ahead)

    def share(c):
        return remote(visitor.at[c], twin.at[c], f_send.at[c], f_recv.at[c], sibling)

    def give(c, k):
        return remote(
            outgoing.at[c, k], incoming.at[c, k], x_send.at[c, k], x_recv.at[c, k], {"frm": peers[k]}
        )

    def pass_on_half(h):
        return remote(upper_half.at[h], visitor_half.at[h], hz_send.at[h], hz_recv.at[h], ahead)

    def share_half(h):
        return remote(visitor_half.at[h], twin_half.at[h], hf_send.at[h], hf_recv.at[h], sibling)

    def give_half(h, k):
        return remote(
            outgoing_half.at[h, k], incoming_half.at[h, k], hx_send.at[h, k], hx_recv.at[h, k], {"frm": peers[k]}
        )

    def rows_of(f, s):
        return pl.ds(pl.multiple_of((f * 2 + s) * rows, rows), rows)

    def share_lower(f):
        return remote(lower.at[rows_of(f, 1 - sub)], lower_twin.at[f], l_send.at[f], l_recv.at[f], sibling)

    def give_sums(k):
        return remote(sums_out.at[k], sums_in.at[k], s_send.at[k], s_recv.at[k], {"frm": peers[k]})

    for i in range(PIECES):
        load_piece(i).start()
    load(1).start()
    barrier = pltpu.get_barrier_semaphore()
    neighbours = [ahead, behind, sibling] + [{"frm": f} for f in peers]
    for device in neighbours:
        pl.semaphore_signal(barrier, inc=1, device_id=device, device_id_type=MESH)

    pick_upper, pick_lower = selector(1), selector(0)

    def separate_upper(c, first, last):
        for g in range(first // GROUP, last // GROUP):
            part = mixed[c, pl.ds(g * GROUP, GROUP)].reshape(2 * GROUP, WIDTH)
            upper[c, pl.ds(g * GROUP, GROUP)] = product(pick_upper, part).astype(jnp.bfloat16)

    for i in range(PIECES):
        load_piece(i).wait()
        separate_upper(0, i * piece, (i + 1) * piece)
        if i == 0:
            pl.semaphore_wait(barrier, len(neighbours))
        pass_on_piece(i).start()
    load(2).start()
    for c in range(1, chunks - 1):
        load(c).wait()
        if c + 2 < chunks:
            load(c + 2).start()
        separate_upper(c, 0, frame_count)
        pass_on(c).start()
    last, middle, half_rows = chunks - 1, frame_count // 2, rows // 2
    load(last).wait()
    for g in range(middle // GROUP):
        early, late = (
            product(pick_upper, mixed[last, pl.ds(first, GROUP)].reshape(2 * GROUP, WIDTH))
            for first in (g * GROUP, middle + g * GROUP)
        )
        upper_half[0, pl.ds(g * GROUP, GROUP)] = joined(early, swapped(late)).astype(jnp.bfloat16)
        upper_half[1, pl.ds(g * GROUP, GROUP)] = joined(swapped(early), late).astype(jnp.bfloat16)
    for h in range(2):
        pass_on_half(h).start()

    def separate(c, _):
        for g in range(frame_count // GROUP):
            part = mixed[c, pl.ds(g * GROUP, GROUP)].reshape(2 * GROUP, WIDTH)
            lower[pl.ds(pl.multiple_of(c * WIDTH, WIDTH), WIDTH), pl.ds(g * GROUP, GROUP)] = (
                product(pick_lower, part).T.astype(jnp.bfloat16)
            )
        return 0

    lax.fori_loop(0, chunks, separate, 0)
    for f in range(n_frm):
        share_lower(f).start()
    for f in range(n_frm):
        share_lower(f).wait_recv()
    ones = jnp.ones((frame_count, 128), jnp.bfloat16)
    for k in range(n_frm - 1):
        sums_out[k] = product(lower[rows_of(peers[k], sub)], ones) + product(lower_twin[peers[k]], ones)
        give_sums(k).start()
    own_sums = product(lower[rows_of(frm, sub)], ones) + product(lower_twin[frm], ones)
    for k in range(n_frm - 1):
        give_sums(k).wait_recv()
        own_sums += sums_in[k]
    mean_lower[...] = own_sums / total

    ones_row = jnp.ones((16, frame_count), jnp.bfloat16)

    def finish(c):
        gram = own[c]
        for k in range(n_frm - 1):
            give(c, k).wait_recv()
            gram += incoming[c, k]
        mean_upper = gram[rows : rows + 1] / total
        out_ref[:, pl.ds(pl.multiple_of(c * WIDTH, WIDTH), WIDTH)] = (
            gram[:rows] / total - mean_lower[...] * mean_upper
        )

    def step(c, _):
        @pl.when(c == 0)
        def _():
            for i in range(PIECES):
                pass_on_piece(i).wait_recv()

        @pl.when(c > 0)
        def _():
            pass_on(c).wait_recv()

        share(c).start()

        for k in range(n_frm - 1):
            outgoing[c, k, :rows] = product(lower[rows_of(peers[k], sub)], visitor[c])
        own[c, :rows] = product(lower[rows_of(frm, sub)], visitor[c])
        share(c).wait_recv()
        column_sums = (product(ones_row, visitor[c]) + product(ones_row, twin[c]))[:SUMS]
        for k in range(n_frm - 1):
            outgoing[c, k, :rows] += product(lower_twin[peers[k]], twin[c])
            outgoing[c, k, rows:] = column_sums
            give(c, k).start()
        own[c, :rows] += product(lower_twin[frm], twin[c])
        own[c, rows:] = column_sums

        @pl.when(c > 0)
        def _():
            finish(c - 1)

        return 0

    lax.fori_loop(0, last, step, 0)

    def step_half(h):
        pass_on_half(h).wait_recv()
        share_half(h).start()

        def folded(left, right):
            early, late = product(left[:, :middle], right), product(left[:, middle:], right)
            return joined(
                early[:half_rows] + swapped(late[:half_rows]), swapped(early[half_rows:]) + late[half_rows:]
            )

        for k in range(n_frm - 1):
            outgoing_half[h, k, :half_rows] = folded(lower[rows_of(peers[k], sub)], visitor_half[h])
        own_half[h, :half_rows] = folded(lower[rows_of(frm, sub)], visitor_half[h])
        share_half(h).wait_recv()
        column_sums = (
            product(ones_row[:, :middle], visitor_half[h]) + product(ones_row[:, :middle], twin_half[h])
        )[:SUMS]
        column_sums = column_sums + swapped(column_sums)
        for k in range(n_frm - 1):
            outgoing_half[h, k, :half_rows] += folded(lower_twin[peers[k]], twin_half[h])
            outgoing_half[h, k, half_rows:] = column_sums
            give_half(h, k).start()
        own_half[h, :half_rows] += folded(lower_twin[frm], twin_half[h])
        own_half[h, half_rows:] = column_sums

    def finished_half(h):
        gram = own_half[h]
        for k in range(n_frm - 1):
            give_half(h, k).wait_recv()
            gram += incoming_half[h, k]
        mean_upper = gram[half_rows : half_rows + 1] / total
        means = joined(mean_lower[:half_rows], mean_lower[half_rows:])
        return gram[:half_rows] / total - means * mean_upper

    step_half(0)
    finish(last - 1)
    step_half(1)
    first_half = finished_half(0)
    second_half = finished_half(1)
    columns = pl.ds(last * WIDTH, WIDTH)
    out_ref[:half_rows, columns] = joined(first_half, swapped(second_half))
    out_ref[half_rows:, columns] = joined(swapped(first_half), second_half)

    for f in range(n_frm):
        share_lower(f).wait_send()
    for k in range(n_frm - 1):
        give_sums(k).wait_send()

    def drain(c, _):
        @pl.when(c == 0)
        def _():
            for i in range(PIECES):
                pass_on_piece(i).wait_send()

        @pl.when(c > 0)
        def _():
            pass_on(c).wait_send()

        share(c).wait_send()
        for k in range(n_frm - 1):
            give(c, k).wait_send()
        return 0

    lax.fori_loop(0, last, drain, 0)
    for h in range(2):
        pass_on_half(h).wait_send()
        share_half(h).wait_send()
        for k in range(n_frm - 1):
            give_half(h, k).wait_send()


def shards(n_pix, n_frm, n_sub, frames):
    frame_count, _, block = frames.shape
    assert n_sub == 2 and block > 2 * WIDTH
    chunks, rows, others = block // WIDTH, block // (n_frm * 2), n_frm - 1
    f32, bf16 = jnp.float32, jnp.bfloat16
    dma = pltpu.SemaphoreType.DMA
    return pl.pallas_call(
        functools.partial(kernel, n_pix, n_frm, max(n_pix // 4, 1)),
        out_shape=jax.ShapeDtypeStruct((rows, block), f32),
        in_specs=[pl.BlockSpec(memory_space=pl.ANY)],
        out_specs=pl.BlockSpec(memory_space=pltpu.VMEM),
        scratch_shapes=[
            pltpu.VMEM((chunks, frame_count, 2, WIDTH), bf16),
            pltpu.VMEM((chunks, frame_count, WIDTH), bf16),
            pltpu.VMEM((chunks, frame_count, WIDTH), bf16),
            pltpu.VMEM((chunks, frame_count, WIDTH), bf16),
            pltpu.VMEM((block, frame_count), bf16),
            pltpu.VMEM((n_frm, rows, frame_count), bf16),
            pltpu.VMEM((chunks, rows + SUMS, WIDTH), f32),
            pltpu.VMEM((chunks, others, rows + SUMS, WIDTH), f32),
            pltpu.VMEM((chunks, others, rows + SUMS, WIDTH), f32),
            pltpu.VMEM((others, rows, 128), f32),
            pltpu.VMEM((others, rows, 128), f32),
            pltpu.VMEM((rows, 128), f32),
            pltpu.VMEM((2, frame_count // 2, WIDTH), bf16),
            pltpu.VMEM((2, frame_count // 2, WIDTH), bf16),
            pltpu.VMEM((2, frame_count // 2, WIDTH), bf16),
            pltpu.VMEM((2, rows // 2 + SUMS, WIDTH), f32),
            pltpu.VMEM((2, others, rows // 2 + SUMS, WIDTH), f32),
            pltpu.VMEM((2, others, rows // 2 + SUMS, WIDTH), f32),
            dma((chunks,)), dma((PIECES,)), dma((PIECES,)), dma((PIECES,)),
            dma((chunks,)), dma((chunks,)), dma((chunks,)), dma((chunks,)),
            dma((chunks, others)), dma((chunks, others)),
            dma((n_frm,)), dma((n_frm,)), dma((others,)), dma((others,)),
            dma((2,)), dma((2,)), dma((2,)), dma((2,)), dma((2, others)), dma((2, others)),
        ],
        compiler_params=pltpu.CompilerParams(
            collective_id=0, has_side_effects=True, vmem_limit_bytes=51 << 20
        ),
        cost_estimate=pl.CostEstimate(
            flops=2 * frame_count * block * block, bytes_accessed=4 * frame_count * block, transcendentals=0
        ),
    )(frames)


def solution(mesh):
    shape = mesh.shape
    return jax.shard_map(
        functools.partial(shards, shape["pix"], shape["frm"], shape["sub"]),
        mesh=mesh,
        in_specs=(P(("grp", "frm", "sub"), None, "pix"),),
        out_specs=P(("grp", "pix", "frm", "sub"), None),
        check_vma=False,
    )
```
